32 devices in a mesh: head: 4 (over x, core), seq: 8 (over z, y).
Axes of the slice: x: 2, y: 2, z: 4, core: 2. Of those that a mesh axis runs over, the one named last changes fastest.
Arguments:
- queries: bfloat16 [4096, 128, 128], P(('seq', 'head')), may hold values from -12 to 12
- keys: bfloat16 [4096, 8, 128], P(('seq', 'head')), may hold values from -7.5 to 7.5
- values: bfloat16 [4096, 8, 128], P(('seq', 'head')), may hold values from -6 to 6
- doc_ids: int32 [4096], replicated, may hold values from 0 to 7, never falling along the last dimension, each value on 1 to 2048 neighbouring positions
Outputs:
- attn_out: bfloat16 [4096, 128, 128], P('seq', 'head')
The draws below stay inside these ranges and needn't reach their ends.
Inputs may be any that keep to these rules, and one draw needn't show every extreme that they name: `doc_ids`: document numbers never fall along the sequence; every document holds 1 to 2048 tokens and one holds exactly 2048.
All inputs are finite; a program needn't handle non-finite values.
Results may differ from the reference program's by a relative error of at most 0.0031.
Values may be sent and summed in bfloat16 or wider, within the bound.
No kernel may reach another device: no remote copies, remote signals or barrier semaphores. Data moves between devices by JAX's collectives and lax.ppermute only.
A program may use at most 128 MiB of HBM per device.

```python
import math
import jax
import jax.numpy as jnp
import numpy as np
from jax import lax

DH = 128
QH = 128
KVH = 8
SEQ_DEV = 512
MAXDOC = 2048
TOKENS = 4096
N_SEQ = 8


def draw_queries(key, part):
    base = 2.0 * jax.random.normal(jax.random.fold_in(key, 1), (TOKENS, QH, DH), jnp.float32)
    base = jnp.clip(base, -12.0, 12.0)
    return base.astype(jnp.bfloat16)


def draw_keys(key, part):
    base = jax.random.normal(jax.random.fold_in(key, 2), (TOKENS, KVH, DH), jnp.float32)
    base = jnp.clip(base, -6.0, 6.0)
    return base.astype(jnp.bfloat16)


def shard_levels(own_key, extent, cuts, least, high):
    def one(dim, blocks):
        heights = jax.random.uniform(jax.random.fold_in(jax.random.fold_in(own_key, 6), dim), (blocks,), jnp.float32, least / len(cuts), high / len(cuts))
        return jnp.repeat(jnp.exp(heights), extent[dim] // blocks).reshape((-1,) + (1,) * (len(extent) - dim - 1))

    factor_of = one(*cuts[0])
    for cut in cuts[1:]:
        factor_of = factor_of * one(*cut)
    return factor_of


def profile(amount, total, limit, lean):
    loads = [(1 << 20) // math.isqrt(grade ** lean) + 1 for grade in range(2, amount + 1)]
    rest, counts = total - limit - (amount - 1), [1] * (amount - 1)
    while rest > 0:
        candidates = [i for i in range(amount - 1) if counts[i] < limit]
        pool, budget = sum([loads[i] for i in candidates]), rest
        for i in candidates:
            addition = min(limit - counts[i], max(1, budget * loads[i] // pool), rest)
            counts[i] = counts[i] + addition
            rest = rest - addition
    return np.array([limit] + counts)


def ragged_sizes(rng, amount, total, bound, slope):
    if amount == 2:
        one = jax.random.randint(rng, (), max(1, total - bound), min(bound, total - 1) + 1)
        return jnp.stack([one, total - one])
    lengths = jnp.asarray(profile(amount, total, bound, slope), jnp.int32)
    twos = (amount - 1) // 2
    source_of, receiver = lengths[1:1 + 2 * twos:2], lengths[2:2 + 2 * twos:2]
    margin = jnp.minimum(source_of - 1, bound - receiver)
    passed = jax.random.randint(jax.random.fold_in(rng, 1), (twos,), 0, 1 << 20) % (margin + 1)
    lengths = lengths.at[1:1 + 2 * twos:2].set(source_of - passed).at[2:2 + 2 * twos:2].set(receiver + passed)
    return lengths[jax.random.permutation(jax.random.fold_in(rng, 2), amount)]


def gaussian(key, shape, spread, reach, cuts=(), kind=jnp.bfloat16):
    level = shard_levels(key, shape, cuts, -0.22, 0.18) if cuts else 1.0
    values = jax.random.normal(key, shape, jnp.float32) * spread * level
    return jnp.minimum(jnp.maximum(values, -reach), reach).astype(kind)


def setup_inputs(seed: int = 0) -> dict:
    arg_keys = jax.random.split(jax.random.key(seed), 5)
    queries = draw_queries(jax.random.fold_in(arg_keys[4], 71), 0)
    keys = draw_keys(jax.random.fold_in(arg_keys[4], 71), 0)
    values = gaussian(arg_keys[2], (TOKENS, KVH, DH), 1.0, 6.0, ((0, 32),))
    doc_ids = jnp.searchsorted(jnp.cumsum(ragged_sizes(arg_keys[3], N_SEQ, TOKENS, MAXDOC, 2)), jnp.arange(TOKENS), side="right").astype(jnp.int32)
    return dict(queries=queries, keys=keys, values=values, doc_ids=doc_ids)


def reference(queries, keys, values, doc_ids):
    head_width = queries.shape[2]
    kv_groups = keys.shape[1]
    per_group = queries.shape[1] // kv_groups
    window = MAXDOC + SEQ_DEV
    blocks = TOKENS // SEQ_DEV
    score_scale = 1.0 / math.sqrt(head_width)
    grouped_q = queries.reshape(TOKENS, kv_groups, per_group, head_width)
    zero_index = jnp.zeros((), jnp.int32)

    def one_block(index):
        block = index // kv_groups
        group = index % kv_groups
        q_start = (block * SEQ_DEV).astype(jnp.int32)
        k_start = jnp.maximum(q_start + SEQ_DEV - window, 0).astype(jnp.int32)
        q_block = lax.dynamic_slice(grouped_q, (q_start, group, zero_index, zero_index), (SEQ_DEV, 1, per_group, head_width))[:, 0].astype(jnp.float32)
        k_block = lax.dynamic_slice(keys, (k_start, group, zero_index), (window, 1, head_width))[:, 0].astype(jnp.float32)
        v_block = lax.dynamic_slice(values, (k_start, group, zero_index), (window, 1, head_width))[:, 0].astype(jnp.float32)
        q_pos = q_start + jnp.arange(SEQ_DEV, dtype=jnp.int32)
        k_pos = k_start + jnp.arange(window, dtype=jnp.int32)
        q_doc = lax.dynamic_slice_in_dim(doc_ids, q_start, SEQ_DEV)
        k_doc = lax.dynamic_slice_in_dim(doc_ids, k_start, window)
        allowed = (q_doc[:, None] == k_doc[None, :]) & (k_pos[None, :] <= q_pos[:, None])
        allowed_b = allowed[:, None, :]
        scores = jnp.einsum('thd,sd->ths', q_block, k_block) * score_scale
        masked = jnp.where(allowed_b, scores, -1e+30)
        top_score = lax.optimization_barrier(jnp.max(masked, axis=-1))
        weights = jnp.where(allowed_b, jnp.exp(masked - top_score[..., None]), 0.0)
        total = lax.optimization_barrier(jnp.sum(weights, axis=-1))
        rounded = lax.optimization_barrier(weights.astype(jnp.bfloat16)).astype(jnp.float32)
        mixed = jnp.einsum('ths,sd->thd', rounded, v_block) / total[..., None]
        return mixed.astype(jnp.bfloat16)
    result = lax.map(one_block, jnp.arange(blocks * kv_groups, dtype=jnp.int32))
    result = result.reshape(blocks, kv_groups, SEQ_DEV, per_group, head_width)
    result = result.transpose(0, 2, 1, 3, 4).reshape(TOKENS, kv_groups * per_group, head_width)
    return result
```

```python
import math

import jax
import jax.numpy as jnp
from jax import lax
from jax.experimental import pallas as pl
from jax.experimental.pallas import tpu as pltpu
from jax.sharding import PartitionSpec as P

MAXDOC = 2048
NEG = -1e30
F32 = jnp.float32
BF16 = jnp.bfloat16


def round_up(value, step):
    return (value + step - 1) // step * step


def fold_rows(op, x):
    out = x[:8]
    for c in range(1, x.shape[0] // 8):
        out = op(out, x[c * 8 : c * 8 + 8])
    return out


def attend_kernel(
    info, start_row, q_ref, *refs, n_blocks, block, piece, tile, big, small, sub, per_group
):
    kv_in = refs[: n_blocks + 1]
    out_ref, k_buf, v_buf, s_buf, m_buf, l_buf, acc, sems = refs[-8:]
    g = pl.program_id(0)
    groups = k_buf.shape[0]
    parts = block // piece
    reach = MAXDOC // block
    exp_scale = math.log2(math.e) / math.sqrt(q_ref.shape[-1])

    def copies(source, slot, sem):
        out = []
        for gg in range(groups):
            for which, buf in ((0, k_buf), (1, v_buf)):
                out.append(
                    pltpu.make_async_copy(
                        source.at[:, which, gg],
                        buf.at[gg, pl.ds(slot * parts, parts)],
                        sems.at[sem, gg * 2 + which],
                    )
                )
        return out

    own, two, four, even_one, even_three, odd_one, odd_three = kv_in

    @pl.when(g == 0)
    def _():
        odd = info[3] == 1
        always = copies(own, reach, 0) + copies(two, reach - 2, 1) + copies(four, reach - 4, 2)
        for c in always:
            c.start()

        @pl.when(odd)
        def _():
            for c in copies(odd_one, reach - 1, 3) + copies(odd_three, reach - 3, 4):
                c.start()
            for c in copies(odd_one, reach - 1, 3) + copies(odd_three, reach - 3, 4):
                c.wait()

        @pl.when(jnp.logical_not(odd))
        def _():
            for c in copies(even_one, reach - 1, 3) + copies(even_three, reach - 3, 4):
                c.start()
            for c in copies(even_one, reach - 1, 3) + copies(even_three, reach - 3, 4):
                c.wait()

        for c in always:
            c.wait()

    lo, hi_start, t0 = info[0], info[1], info[2]
    base = t0 // 128 * 128
    rows = tile * per_group
    sub_tokens = sub // per_group

    def keys_of(buf, u0, n):
        return buf[g, pl.ds(u0 // piece, n // piece)].reshape(n, buf.shape[-1])

    def scores_step(u0, n, kind):
        u0 = pl.multiple_of(u0, 128)
        c0 = pl.multiple_of(u0 - base + MAXDOC, 128)
        kk = keys_of(k_buf, u0, n)
        for i in range(rows // sub):
            r = pl.ds(i * sub, sub)
            q = q_ref[pl.ds(i * sub_tokens, sub_tokens)].reshape(sub, q_ref.shape[-1])
            s = lax.dot_general(kk, q, (((1,), (1,)), ((), ())), preferred_element_type=F32)
            if kind != "full":
                u = u0 + lax.broadcasted_iota(jnp.int32, (n, sub), 0)
                ok = u >= start_row[:, r]
                if kind == "diagonal":
                    lane = lax.broadcasted_iota(jnp.int32, (1, sub), 1)
                    ok = ok & (u <= t0 + i * sub_tokens + lane // per_group)
                s = jnp.where(ok, s, NEG)
            s_buf[pl.ds(c0, n), r] = s
            top = fold_rows(jnp.maximum, s)
            m_buf[:, r] = top if kind == "diagonal" else jnp.maximum(m_buf[:, r], top)

    def values_step(u0, n, kind):
        u0 = pl.multiple_of(u0, 128)
        c0 = pl.multiple_of(u0 - base + MAXDOC, 128)
        vv = keys_of(v_buf, u0, n)
        for i in range(rows // sub):
            r = pl.ds(i * sub, sub)
            p = jnp.exp2(s_buf[pl.ds(c0, n), r] * exp_scale - m_buf[0:1, r])
            pv = lax.dot_general(
                vv, p.astype(BF16), (((0,), (0,)), ((), ())), preferred_element_type=F32
            )
            total = fold_rows(jnp.add, p)
            if kind == "diagonal":
                acc[:, r] = pv
                l_buf[:, r] = total
            else:
                acc[:, r] = acc[:, r] + pv
                l_buf[:, r] = l_buf[:, r] + total

    diagonal = max(128, tile)
    n_full = jnp.maximum(base - hi_start, 0) // big
    edge = base - n_full * big
    n_masked = (jnp.maximum(edge - lo, 0) + small - 1) // small

    def all_steps(step):
        step(base, diagonal, "diagonal")

        def full(j, carry):
            step(base - (j + 1) * big, big, "full")
            return carry

        def masked(j, carry):
            step(edge - (j + 1) * small, small, "masked")
            return carry

        lax.fori_loop(0, n_full, full, 0)
        lax.fori_loop(0, n_masked, masked, 0)

    all_steps(scores_step)
    m_buf[0:1, :] = jnp.max(m_buf[...], axis=0, keepdims=True) * exp_scale
    all_steps(values_step)
    for i in range(rows // sub):
        r = pl.ds(i * sub, sub)
        inverse = 1.0 / jnp.sum(l_buf[:, r], axis=0, keepdims=True)
        o = (acc[:, r] * inverse).astype(BF16).T
        out_ref[pl.ds(i * sub_tokens, sub_tokens)] = o.reshape(sub_tokens, per_group, o.shape[-1])


def attend(info, start_row, q, head_block, token_block, kv_blocks, out, local_heads):
    tile, width = q.shape[0], q.shape[-1]
    parts, _, groups, piece, _ = kv_blocks[0].shape
    block = parts * piece
    per_group = local_heads // groups
    rows = tile * per_group
    reach = MAXDOC // block
    keys = (reach + 1) * block
    n_blocks = len(kv_blocks) - 1
    sub = min(512, rows)
    scalars = jnp.concatenate([info, jnp.stack([head_block, token_block]).astype(jnp.int32)])

    def kernel(*refs):
        attend_kernel(
            *refs,
            n_blocks=n_blocks,
            block=block,
            piece=piece,
            tile=tile,
            big=512,
            small=256,
            sub=sub,
            per_group=per_group,
        )

    any_spec = pl.BlockSpec(memory_space=pl.ANY)
    grid_spec = pltpu.PrefetchScalarGridSpec(
        num_scalar_prefetch=1,
        grid=(groups,),
        in_specs=[
            pl.BlockSpec((1, rows), lambda g, s: (0, s[5])),
            pl.BlockSpec((tile, per_group, width), lambda g, s: (0, s[4] * groups + g, 0)),
        ]
        + [any_spec] * (len(kv_blocks) + (out is not None)),
        out_specs=pl.BlockSpec((tile, per_group, width), lambda g, s: (s[5], g, 0)),
        scratch_shapes=[
            pltpu.VMEM((groups, keys // piece, piece, width), BF16),
            pltpu.VMEM((groups, keys // piece, piece, width), BF16),
            pltpu.VMEM((MAXDOC + max(128, tile), rows), F32),
            pltpu.VMEM((8, rows), F32),
            pltpu.VMEM((8, rows), F32),
            pltpu.VMEM((width, rows), F32),
            pltpu.SemaphoreType.DMA((5, 2 * groups)),
        ],
    )
    return pl.pallas_call(
        kernel,
        grid_spec=grid_spec,
        out_shape=jax.ShapeDtypeStruct((block, local_heads, width), BF16),
        input_output_aliases={} if out is None else {3 + len(kv_blocks): 0},
        compiler_params=pltpu.CompilerParams(vmem_limit_bytes=48 * 2**20),
        cost_estimate=pl.CostEstimate(
            flops=rows * groups * MAXDOC * width * 4,
            bytes_accessed=8 * 2**20,
            transcendentals=rows * groups * MAXDOC,
        ),
    )(scalars, start_row, q, *kv_blocks, *([] if out is None else [out]))


def shift(x, distance, only=None):
    n = lax.axis_size("seq")
    route = [
        (i, i + distance)
        for i in range(n)
        if 0 <= i + distance < n and (only is None or i % 2 == only)
    ]
    return lax.ppermute(x, "seq", route)


def swap_pairs(x):
    n = lax.axis_size("seq")
    return lax.ppermute(x, "seq", [(i, i ^ 1) for i in range(n) if i ^ 1 < n])


def per_device(queries, keys, values, doc_ids):
    seq_index = lax.axis_index("seq")
    head_index = lax.axis_index("head")
    n_head = lax.axis_size("head")
    tile, q_heads, width = queries.shape
    kv_heads = keys.shape[1]
    groups = kv_heads // n_head
    local_heads = q_heads // n_head
    per_group = local_heads // groups
    block = tile * n_head
    reach = MAXDOC // block

    packed = jnp.stack([keys, values]).reshape(2, tile, n_head, groups, width)
    packed = packed.transpose(2, 0, 3, 1, 4)
    own = lax.all_to_all(packed, "head", 0, 0, tiled=True)

    two = shift(own, 2)
    odd_one = shift(own, 1, only=0)
    four = shift(two, 2)
    swapped = swap_pairs(two)
    even_three = shift(four, -1, only=1)
    blocks = (own, two, four, swapped, even_three, odd_one, swapped)

    q_doc = lax.dynamic_slice_in_dim(doc_ids, seq_index * block, block)
    start = jnp.sum((doc_ids[None, :] < q_doc[:, None]).astype(jnp.int32), axis=1)
    start = start - (seq_index - reach) * block
    start_row = jnp.repeat(start, per_group)[None]
    odd = (seq_index % 2).astype(jnp.int32)

    out = None
    for d in range(n_head):
        partner = head_index ^ d
        if d == 0:
            q, head_block = queries, head_index
        else:
            q = lax.dynamic_slice_in_dim(queries, partner * local_heads, local_heads, axis=1)
            q = lax.ppermute(q, "head", [(i, i ^ d) for i in range(n_head)])
            head_block = jnp.int32(0)
        first = partner * tile
        info = jnp.stack(
            [start[first], start[first + tile - 1], reach * block + first, odd]
        ).astype(jnp.int32)
        out = attend(info, start_row, q, head_block, partner, blocks, out, local_heads)
    return out


def solution(mesh):
    in_specs = (
        P(("seq", "head"), None, None),
        P(("seq", "head"), None, None),
        P(("seq", "head"), None, None),
        P(),
    )
    out_specs = P("seq", "head", None)
    return jax.shard_map(
        per_device, mesh=mesh, in_specs=in_specs, out_specs=out_specs, check_vma=False
    )
```

```python
import math

import jax
import jax.numpy as jnp
from jax import lax
from jax.experimental import pallas as pl
from jax.experimental.pallas import tpu as pltpu
from jax.sharding import PartitionSpec as P

MAXDOC = 2048
STEP = 512
EXTRA = 16
NEG = -1e30
F32 = jnp.float32
BF16 = jnp.bfloat16


def round_up(value, step):
    return (value + step - 1) // step * step


def fold_rows(op, x):
    out = x[:8]
    for c in range(1, x.shape[0] // 8):
        out = op(out, x[c * 8 : c * 8 + 8])
    return out


def attend_kernel(info, *refs, n_q, n_kv, n_groups, count, width):
    start_ref = refs[0]
    q_in = refs[1 : 1 + n_q]
    own, two, four, even_one, even_three, odd_one, odd_three = refs[1 + n_q : 1 + n_q + n_kv]
    out_ref = refs[1 + n_q + n_kv]
    q_buf, k_buf, v_buf, vt_buf, s_buf, p_buf, m_buf, m_old, f_buf, acc, o_buf, sems, q_sems, o_sems = (
        refs[2 + n_q + n_kv :]
    )
    tile, per_group = q_buf.shape[1], q_buf.shape[2]
    rows = tile * per_group
    n_head, _, _, piece, _ = own.shape
    block = n_head * piece
    reach = MAXDOC // block
    pad = STEP // piece
    col = min(256, rows)
    chunk = 128
    col_tokens = col // per_group
    exp_scale = math.log2(math.e) / math.sqrt(width)
    odd = info[0] % 2 == 1
    head = info[1]

    def copies(source, slot, sem):
        return [
            pltpu.make_async_copy(
                source.at[:, which, g],
                buf.at[g, pl.ds(pad + slot * n_head, n_head)],
                sems.at[sem, g * 2 + which],
            )
            for g in range(n_groups)
            for which, buf in ((0, k_buf), (1, v_buf))
        ]

    q_copies = []
    for t in range(count):
        source, g = q_in[t // n_groups], t % n_groups
        part = (head, 0, head % 2, 0)[min(t // n_groups, 2) + (t // n_groups > 2 and t // n_groups % 2)]
        first_head = part * n_groups * per_group
        q_copies.append(
            pltpu.make_async_copy(
                source.at[:, pl.ds(first_head + g * per_group, per_group)], q_buf.at[t], q_sems.at[t]
            )
        )
    always = copies(own, reach, 0) + copies(two, reach - 2, 1) + copies(four, reach - 4, 2)
    for c in always + q_copies:
        c.start()
    at_odd = copies(odd_one, reach - 1, 3) + copies(odd_three, reach - 3, 4)
    at_even = copies(even_one, reach - 1, 3) + copies(even_three, reach - 3, 4)
    for wanted, parity in ((at_odd, odd), (at_even, jnp.logical_not(odd))):

        @pl.when(parity)
        def _():
            for c in wanted:
                c.start()

    v_buf[:, 0:pad] = jnp.zeros((n_groups, pad, piece, width), BF16)
    s_buf[...] = jnp.full(s_buf.shape, NEG, F32)
    p_buf[...] = jnp.zeros(p_buf.shape, BF16)
    for buf in (m_buf, m_old, acc):
        buf[...] = jnp.zeros(buf.shape, F32)
    f_buf[...] = jnp.ones(f_buf.shape, F32)
    vt_buf[:, width:, :] = jnp.ones((n_groups, EXTRA, vt_buf.shape[2]), BF16)
    for c in at_even:
        c.wait()
    for c in always + q_copies:
        c.wait()
    for g in range(n_groups):
        for b in range(v_buf.shape[1] * piece // STEP):
            part = v_buf[g, b * pad : (b + 1) * pad].reshape(STEP, width)
            vt_buf[g, 0:width, b * STEP : (b + 1) * STEP] = part.T

    def facts(t):
        first = (head ^ (t // n_groups)) * tile
        t0 = reach * block + first
        top = (t0 + tile + 127) // 128 * 128
        return first, t0, top, info[2 + first], info[2 + first + tile - 1]

    def n_steps(t):
        _, _, top, lo, _ = facts(t)
        return (top - lo + STEP - 1) // STEP

    def key_of(t, j):
        return facts(t)[2] - (j + 1) * STEP

    def body(qk, ex, pv, masked):
        (t, j), (_, _), (t2, j2) = qk, ex, pv
        first, t0, _, _, _ = facts(t)
        g, g2 = t % n_groups, t2 % n_groups
        u0 = key_of(t, j)
        k_first = (u0 + STEP) // piece
        v_first = pl.multiple_of(key_of(t2, j2) + STEP, 128)
        vt = vt_buf[g2, :, pl.ds(v_first, STEP)]
        opening = j == 0
        for b in range(rows // col):
            r = pl.ds(b * col, col)
            f = f_buf[:, r]
            acc[:, r] = acc[:, r] * f + jnp.dot(vt, p_buf[:, r], preferred_element_type=F32)
            m = m_buf[:, r]
            f_buf[:, r] = jnp.exp2(m_old[:, r] - m)
            q = q_buf[t, pl.ds(b * col_tokens, col_tokens)].reshape(col, width)
            top = None
            for a in range(STEP // chunk):
                k = pl.ds(a * chunk, chunk)
                p = jnp.exp2(s_buf[k, r] * exp_scale - m)
                p_buf[k, r] = p.astype(BF16)
                kk = k_buf[g, pl.ds(k_first + a * (chunk // piece), chunk // piece)].reshape(chunk, width)
                s = lax.dot_general(kk, q, (((1,), (1,)), ((), ())), preferred_element_type=F32)
                if masked:
                    u = u0 + a * chunk + lax.broadcasted_iota(jnp.int32, (chunk, col), 0)
                    lane = lax.broadcasted_iota(jnp.int32, (1, col), 1)
                    at = t0 + b * col_tokens + lane // per_group
                    ok = (u >= start_ref[first // tile, :, r]) & (u <= at)
                    s = jnp.where(ok, s, NEG)
                s_buf[k, r] = s
                part = fold_rows(jnp.maximum, s)
                top = part if top is None else jnp.maximum(top, part)
            before = jnp.where(opening, NEG, m)
            m_old[:, r] = before
            m_buf[:, r] = jnp.maximum(before, jnp.max(top, axis=0, keepdims=True) * exp_scale)

    def finish(t):
        for b in range(rows // col):
            r = pl.ds(b * col, col)
            inverse = 1.0 / acc[width : width + 1, r]
            o = (acc[0:width, r] * inverse).astype(BF16).T
            o_buf[t, pl.ds(b * col_tokens, col_tokens)] = o.reshape(col_tokens, per_group, width)
        o_copy(t).start()

    def o_copy(t):
        return pltpu.make_async_copy(
            o_buf.at[t],
            out_ref.at[
                pl.ds(facts(t)[0], tile), pl.ds((t % n_groups) * per_group, per_group)
            ],
            o_sems.at[t],
        )

    total_steps = n_steps(0)
    for t in range(1, count):
        total_steps = total_steps + n_steps(t)

    def loop(s, carry):
        t, j, t1, j1, t2, j2 = carry
        _, _, top, _, hi_start = facts(t)
        masked = (j == 0) | (top - (j + 1) * STEP < hi_start)

        @pl.when(masked)
        def _():
            body((t, j), (t1, j1), (t2, j2), True)

        @pl.when(jnp.logical_not(masked))
        def _():
            body((t, j), (t1, j1), (t2, j2), False)

        @pl.when((s >= 2) & (j2 == n_steps(t2) - 1))
        def _():
            finish(t2)

        over = j == n_steps(t) - 1
        t_next = jnp.where(over, jnp.minimum(t + 1, count - 1), t)
        j_next = jnp.where(over, 0, j + 1)
        return t_next, j_next, t, j, t1, j1

    zero = jnp.int32(0)
    lax.fori_loop(0, total_steps + 2, loop, (zero,) * 6)
    for t in range(count):
        o_copy(t).wait()


def attend(info, start_row, qs, n_groups, kv_blocks, local_heads):
    tile, _, width = qs[0].shape
    n_head, _, _, piece, _ = kv_blocks[0].shape
    block = n_head * piece
    per_group = local_heads // n_groups
    rows = tile * per_group
    keys = MAXDOC + block + STEP
    count = len(qs) * n_groups

    def kernel(*refs):
        attend_kernel(
            *refs,
            n_q=len(qs),
            n_kv=len(kv_blocks),
            n_groups=n_groups,
            count=count,
            width=width,
        )

    any_spec = pl.BlockSpec(memory_space=pl.ANY)
    grid_spec = pltpu.PrefetchScalarGridSpec(
        num_scalar_prefetch=1,
        grid=(1,),
        in_specs=[pl.BlockSpec(memory_space=pltpu.VMEM)]
        + [any_spec] * (len(qs) + len(kv_blocks)),
        out_specs=any_spec,
        scratch_shapes=[
            pltpu.VMEM((count, tile, per_group, width), BF16),
            pltpu.VMEM((n_groups, keys // piece, piece, width), BF16),
            pltpu.VMEM((n_groups, keys // piece, piece, width), BF16),
            pltpu.VMEM((n_groups, width + EXTRA, keys), BF16),
            pltpu.VMEM((STEP, rows), F32),
            pltpu.VMEM((STEP, rows), BF16),
            pltpu.VMEM((1, rows), F32),
            pltpu.VMEM((1, rows), F32),
            pltpu.VMEM((1, rows), F32),
            pltpu.VMEM((width + EXTRA, rows), F32),
            pltpu.VMEM((count, tile, per_group, width), BF16),
            pltpu.SemaphoreType.DMA((5, 2 * n_groups)),
            pltpu.SemaphoreType.DMA((count,)),
            pltpu.SemaphoreType.DMA((count,)),
        ],
    )
    return pl.pallas_call(
        kernel,
        grid_spec=grid_spec,
        out_shape=jax.ShapeDtypeStruct((block, local_heads, width), BF16),
        compiler_params=pltpu.CompilerParams(vmem_limit_bytes=60 * 2**20),
        cost_estimate=pl.CostEstimate(flops=2**20, bytes_accessed=2**20, transcendentals=0),
    )(info, start_row, *qs, *kv_blocks)


def assemble(ids, pieces):
    n = len(pieces)

    def kernel(ids, *refs):
        for d in range(n):
            refs[n][ids[1] ^ d] = refs[d][...]

    return pl.pallas_call(
        kernel,
        grid_spec=pltpu.PrefetchScalarGridSpec(
            num_scalar_prefetch=1,
            grid=(1,),
            in_specs=[pl.BlockSpec(memory_space=pltpu.VMEM)] * n,
            out_specs=pl.BlockSpec(memory_space=pltpu.VMEM),
        ),
        out_shape=jax.ShapeDtypeStruct((n, *pieces[0].shape), BF16),
    )(ids, *pieces)


def exchange(x, distance):
    n = lax.axis_size("head")
    return lax.ppermute(x, "head", [(i, i ^ distance) for i in range(n)])


def shift(x, distance, only=None):
    n = lax.axis_size("seq")
    route = [
        (i, i + distance)
        for i in range(n)
        if 0 <= i + distance < n and (only is None or i % 2 == only)
    ]
    return lax.ppermute(x, "seq", route)


def swap_pairs(x):
    n = lax.axis_size("seq")
    return lax.ppermute(x, "seq", [(i, i ^ 1) for i in range(n) if i ^ 1 < n])


def per_device(queries, keys, values, doc_ids):
    seq_index = lax.axis_index("seq")
    head_index = lax.axis_index("head")
    n_head = lax.axis_size("head")
    tile, q_heads, width = queries.shape
    kv_heads = keys.shape[1]
    groups = kv_heads // n_head
    local_heads = q_heads // n_head
    per_group = local_heads // groups
    block = tile * n_head
    reach = MAXDOC // block

    packed = jnp.stack([keys, values]).reshape(2, tile, n_head, groups, width)
    packed = packed.transpose(2, 0, 3, 1, 4)
    info_ids = jnp.stack([seq_index, head_index]).astype(jnp.int32)
    pieces = [lax.dynamic_index_in_dim(packed, head_index ^ d, 0, keepdims=False) for d in range(n_head)]
    pieces = [piece if d == 0 else exchange(piece, d) for d, piece in enumerate(pieces)]
    near = lax.dynamic_slice_in_dim(queries, (head_index ^ 1) * local_heads, local_heads, axis=1)
    pairs = [
        lax.dynamic_slice_in_dim(
            queries, (head_index ^ d) // 2 * 2 * local_heads, 2 * local_heads, axis=1
        )
        for d in range(2, n_head, 2)
    ]
    pieces, near, pairs = lax.optimization_barrier((pieces, near, pairs))
    own = assemble(info_ids, pieces)

    two = shift(own, 2)
    odd_one = shift(own, 1, only=0)
    four = shift(two, 2)
    swapped = swap_pairs(two)
    even_three = shift(four, -1, only=1)
    blocks = (own, two, four, swapped, even_three, odd_one, swapped)

    q_doc = lax.dynamic_slice_in_dim(doc_ids, seq_index * block, block)
    start = jnp.sum((doc_ids[None, :] < q_doc[:, None]).astype(jnp.int32), axis=1)
    start = start - (seq_index - reach) * block
    start_row = jnp.repeat(start, per_group).reshape(n_head, 1, tile * per_group)
    info = jnp.concatenate([info_ids, start])

    arrived = [queries, exchange(near, 1)]
    for d, pair in zip(range(2, n_head, 2), pairs):
        pair = exchange(pair, d)
        other = lax.dynamic_slice_in_dim(
            pair, (1 - head_index % 2) * local_heads, local_heads, axis=1
        )
        other, _ = lax.optimization_barrier((other, blocks))
        arrived += [pair, exchange(other, 1)]
    out = attend(info, start_row, arrived, groups, blocks, local_heads)
    return out


def solution(mesh):
    in_specs = (
        P(("seq", "head"), None, None),
        P(("seq", "head"), None, None),
        P(("seq", "head"), None, None),
        P(),
    )
    out_specs = P("seq", "head", None)
    return jax.shard_map(
        per_device, mesh=mesh, in_specs=in_specs, out_specs=out_specs, check_vma=False
    )
```

```python
import math

import jax
import jax.numpy as jnp
from jax import lax
from jax.experimental import pallas as pl
from jax.experimental.pallas import tpu as pltpu
from jax.sharding import PartitionSpec as P

MAXDOC = 2048
EXTRA = 16
NEG = -1e30
F32 = jnp.float32
BF16 = jnp.bfloat16


def round_up(value, step):
    return (value + step - 1) // step * step


def fold_rows(op, x):
    out = x[:8]
    for c in range(1, x.shape[0] // 8):
        out = op(out, x[c * 8 : c * 8 + 8])
    return out


def attend_kernel(info, *refs, n_q, n_kv, n_carried, last, n_groups, width):
    count = n_q * n_groups
    refs = list(refs)
    start_ref = refs.pop(0)
    q_in = [refs.pop(0) for _ in range(n_q)]
    kv_in = [refs.pop(0) for _ in range(n_kv)]
    state_in = [refs.pop(0) for _ in range(2 if n_carried else 0)]
    out_refs = [refs.pop(0) for _ in range(1 if last else 2)]
    q_buf, k_buf, v_buf, vt_buf, s_buf, p_buf, m_buf, m_old, m_in, f_buf, acc, state, o_buf, sems, q_sems, o_sems = refs
    tile, per_group = q_buf.shape[1], q_buf.shape[2]
    rows = tile * per_group
    n_head, _, _, piece, _ = kv_in[0].shape
    block = n_head * piece
    reach = MAXDOC // block
    col = min(256, rows)
    chunk = 128
    col_tokens = col // per_group
    exp_scale = math.log2(math.e) / math.sqrt(width)
    odd = info[0] % 2 == 1
    head = info[1]

    def copies(source, slot, sem):
        return [
            pltpu.make_async_copy(
                source.at[:, which, g],
                buf.at[g, pl.ds((slot + 1) * n_head, n_head)],
                sems.at[sem, g * 2 + which],
            )
            for g in range(n_groups)
            for which, buf in ((0, k_buf), (1, v_buf))
        ]

    loads, later = [], []
    for t in range(count):
        source, g = q_in[t // n_groups], t % n_groups
        part = (head, 0, head % 2, 0)[min(t // n_groups, 2) + (t // n_groups > 2 and t // n_groups % 2)]
        first_head = part * n_groups * per_group + g * per_group
        later.append(
            pltpu.make_async_copy(
                source.at[:, pl.ds(first_head, per_group)], q_buf.at[t], q_sems.at[0, t]
            )
        )
    loads += copies(kv_in[0], reach, 0) + copies(kv_in[1], reach - 2, 1)
    at_odd = copies(kv_in[2], reach - 1, 2)
    at_even = []
    slots = [reach, reach - 1, reach - 2]
    if last:
        four, swapped, even_three = kv_in[3:]
        loads += copies(four, reach - 4, 3)
        at_odd += copies(swapped, reach - 3, 4)
        at_even += copies(swapped, reach - 1, 2) + copies(even_three, reach - 3, 4)
        slots = range(reach + 1)

    def sums_of(t):
        return pltpu.make_async_copy(state_in[0].at[t], state.at[t], q_sems.at[1, t])

    m_in[...] = jnp.full(m_in.shape, NEG, F32)
    if n_carried:
        loads.append(
            pltpu.make_async_copy(state_in[1], m_in.at[pl.ds(0, n_carried)], sems.at[5, 0])
        )
        later = [c for t, q in enumerate(later) for c in [q] + ([sums_of(t)] if t < n_carried else [])]
    for c in loads:
        c.start()
    for wanted, parity in ((at_odd, odd), (at_even, jnp.logical_not(odd))):

        @pl.when(parity)
        def _():
            for c in wanted:
                c.start()

    for c in later:
        c.start()
    s_buf[...] = jnp.full(s_buf.shape, NEG, F32)
    p_buf[...] = jnp.zeros(p_buf.shape, BF16)
    for buf in (m_buf, m_old, acc):
        buf[...] = jnp.zeros(buf.shape, F32)
    f_buf[...] = jnp.ones(f_buf.shape, F32)
    vt_buf[:, width:, :] = jnp.ones((n_groups, EXTRA, vt_buf.shape[2]), BF16)
    vt_buf[:, :, 0:block] = jnp.zeros((n_groups, width + EXTRA, block), BF16)
    for wanted, parity in ((at_odd, odd), (at_even, jnp.logical_not(odd))):

        @pl.when(parity)
        def _():
            for c in wanted:
                c.wait()

    for c in loads:
        c.wait()
    for g in range(n_groups):
        for b in slots:
            part = v_buf[g, (b + 1) * n_head : (b + 2) * n_head].reshape(block, width)
            vt_buf[g, 0:width, (b + 1) * block : (b + 2) * block] = part.T
    if n_carried:
        sums_of(0).wait()
        acc[...] = state[0]

    def first_of(t):
        return (head ^ (t // n_groups)) * tile

    def n_steps(t):
        back = reach - info[2 + first_of(t)] // block
        if not last:
            return 1 + jnp.where(odd, jnp.minimum(back, 2), jnp.minimum(back // 2, 1))
        n_even = jnp.where(back >= 3, back - 1, jnp.minimum(back, 1))
        carried = jnp.maximum(jnp.where(odd, back - 2, n_even), 1)
        below_top = top_of(t) - info[2 + first_of(t)]
        return jnp.where(t < n_carried, carried, (below_top + block - 1) // block)

    def top_of(t):
        return (reach * block + first_of(t) + tile + 127) // 128 * 128

    def key_of(t, j):
        if not last:
            return (reach - jnp.where(odd, j, 2 * j)) * block
        back = jnp.where(odd, j + 3, jnp.where(j == 0, 1, j + 2))
        return jnp.where(t < n_carried, (reach - back) * block, top_of(t) - (j + 1) * block)

    def body(qk, ex, pv, mask):
        (t, j), (_, _), (t2, j2) = qk, ex, pv
        first = first_of(t)
        g, g2 = t % n_groups, t2 % n_groups
        u0 = key_of(t, j)
        k_first = (u0 + block) // piece
        v_first = pl.multiple_of(key_of(t2, j2) + block, 128)
        vt = vt_buf[g2, :, pl.ds(v_first, block)]
        opening = j == 0
        for b in range(rows // col):
            r = pl.ds(b * col, col)
            f = f_buf[:, r]
            acc[:, r] = acc[:, r] * f + jnp.dot(vt, p_buf[:, r], preferred_element_type=F32)
            m = m_buf[:, r]
            f_buf[:, r] = jnp.exp2(m_old[:, r] - m)
            q = q_buf[t, pl.ds(b * col_tokens, col_tokens)].reshape(col, width)
            top = None
            for a in range(block // chunk):
                k = pl.ds(a * chunk, chunk)
                p = jnp.exp2(s_buf[k, r] * exp_scale - m)
                p_buf[k, r] = p.astype(BF16)
                per = chunk // piece
                kk = k_buf[g, pl.ds(k_first + a * per, per)].reshape(chunk, width)
                s = lax.dot_general(kk, q, (((1,), (1,)), ((), ())), preferred_element_type=F32)
                if mask != "none":
                    u = a * chunk + lax.broadcasted_iota(jnp.int32, (chunk, col), 0)
                    lane = lax.broadcasted_iota(jnp.int32, (1, col), 1)
                    at = reach * block + first - u0 + b * col_tokens + lane // per_group
                    ok = u <= at
                    if mask == "start":
                        ok = ok & (u >= start_ref[first // tile, :, r] - u0)
                    s = jnp.where(ok, s, NEG)
                s_buf[k, r] = s
                part = fold_rows(jnp.maximum, s)
                top = part if top is None else jnp.maximum(top, part)
            before = jnp.where(opening, m_in[t, :, r], m)
            m_old[:, r] = before
            m_buf[:, r] = jnp.maximum(before, jnp.max(top, axis=0, keepdims=True) * exp_scale)

    def results(t):
        if not last:
            return [
                pltpu.make_async_copy(state.at[t], out_refs[0].at[t], o_sems.at[0, t]),
                pltpu.make_async_copy(m_in.at[t], out_refs[1].at[t], o_sems.at[1, t]),
            ]
        heads = pl.ds((t % n_groups) * per_group, per_group)
        target = out_refs[0].at[pl.ds(first_of(t), tile), heads]
        return [pltpu.make_async_copy(o_buf.at[t], target, o_sems.at[0, t])]

    def finish(t, top):
        if last:
            for b in range(rows // col):
                r = pl.ds(b * col, col)
                inverse = 1.0 / acc[width : width + 1, r]
                o = (acc[0:width, r] * inverse).astype(BF16).T
                o_buf[t, pl.ds(b * col_tokens, col_tokens)] = o.reshape(col_tokens, per_group, width)
            if n_carried:

                @pl.when(t + 1 < n_carried)
                def _():
                    sums_of(t + 1).wait()
                    acc[...] = state[t + 1]
        else:
            state[t] = acc[...]
        for c in results(t):
            c.start()

    total_steps = n_steps(0)
    for t in range(1, count):
        total_steps = total_steps + n_steps(t)

    def loop(s, carry):
        t, j, t1, j1, t2, j2 = carry
        hi_start = info[2 + first_of(t) + tile - 1]
        at_start = key_of(t, j) < hi_start
        at_end = key_of(t, j) + block > reach * block + first_of(t)
        cases = {
            "start": at_start,
            "diagonal": jnp.logical_not(at_start) & at_end,
            "none": jnp.logical_not(at_start) & jnp.logical_not(at_end),
        }
        if not last:
            @pl.when((s >= 1) & (j1 == n_steps(t1) - 1))
            def _():
                m_in[t1] = m_buf[...]

        @pl.when((j == 0) & (s < total_steps))
        def _():
            pltpu.make_async_copy(
                q_in[0].at[:, pl.ds(0, per_group)], q_buf.at[t], q_sems.at[0, t]
            ).wait()

        for mask, case in cases.items():

            @pl.when(case)
            def _():
                body((t, j), (t1, j1), (t2, j2), mask)

        @pl.when((s >= 2) & (j2 == n_steps(t2) - 1))
        def _():
            finish(t2, None)

        over = j == n_steps(t) - 1
        t_next = jnp.where(over, jnp.minimum(t + 1, count - 1), t)
        j_next = jnp.where(over, 0, j + 1)
        return t_next, j_next, t, j, t1, j1

    zero = jnp.int32(0)
    lax.fori_loop(0, total_steps + 2, loop, (zero,) * 6)
    for t in range(count):
        for c in results(t):
            c.wait()


def attend(info, start_row, qs, n_groups, kv_blocks, state, last, local_heads):
    tile, _, width = qs[0].shape
    n_head, _, _, piece, _ = kv_blocks[0].shape
    block = n_head * piece
    per_group = local_heads // n_groups
    rows = tile * per_group
    keys = MAXDOC + 2 * block
    count = len(qs) * n_groups
    n_carried = state[0].shape[0] if state else 0
    n_state = n_carried if last else count

    def kernel(*refs):
        attend_kernel(
            *refs,
            n_q=len(qs),
            n_kv=len(kv_blocks),
            n_carried=n_carried,
            last=last,
            n_groups=n_groups,
            width=width,
        )

    any_spec = pl.BlockSpec(memory_space=pl.ANY)
    if last:
        out_shape = jax.ShapeDtypeStruct((block, local_heads, width), BF16)
    else:
        out_shape = (
            jax.ShapeDtypeStruct((count, width + EXTRA, rows), F32),
            jax.ShapeDtypeStruct((count, 1, rows), F32),
        )
    grid_spec = pltpu.PrefetchScalarGridSpec(
        num_scalar_prefetch=1,
        grid=(1,),
        in_specs=[pl.BlockSpec(memory_space=pltpu.VMEM)]
        + [any_spec] * (len(qs) + len(kv_blocks) + len(state)),
        out_specs=any_spec if last else (any_spec, any_spec),
        scratch_shapes=[
            pltpu.VMEM((count, tile, per_group, width), BF16),
            pltpu.VMEM((n_groups, keys // piece, piece, width), BF16),
            pltpu.VMEM((n_groups, keys // piece, piece, width), BF16),
            pltpu.VMEM((n_groups, width + EXTRA, keys), BF16),
            pltpu.VMEM((block, rows), F32),
            pltpu.VMEM((block, rows), BF16),
            pltpu.VMEM((1, rows), F32),
            pltpu.VMEM((1, rows), F32),
            pltpu.VMEM((count, 1, rows), F32),
            pltpu.VMEM((1, rows), F32),
            pltpu.VMEM((width + EXTRA, rows), F32),
            pltpu.VMEM((n_state, width + EXTRA, rows), F32),
            pltpu.VMEM((count, tile, per_group, width), BF16),
            pltpu.SemaphoreType.DMA((6, 2 * n_groups)),
            pltpu.SemaphoreType.DMA((2, count)),
            pltpu.SemaphoreType.DMA((2, count)),
        ],
    )
    return pl.pallas_call(
        kernel,
        grid_spec=grid_spec,
        out_shape=out_shape,
        compiler_params=pltpu.CompilerParams(vmem_limit_bytes=63 * 2**20),
        cost_estimate=pl.CostEstimate(
            flops=2**20 if last else 6 * 10**9, bytes_accessed=2**20, transcendentals=0
        ),
    )(info, start_row, *qs, *kv_blocks, *state)


def assemble(ids, pieces):
    n = len(pieces)

    def kernel(ids, *refs):
        for d in range(n):
            refs[n][ids[1] ^ d] = refs[d][...]

    return pl.pallas_call(
        kernel,
        grid_spec=pltpu.PrefetchScalarGridSpec(
            num_scalar_prefetch=1,
            grid=(1,),
            in_specs=[pl.BlockSpec(memory_space=pltpu.VMEM)] * n,
            out_specs=pl.BlockSpec(memory_space=pltpu.VMEM),
        ),
        out_shape=jax.ShapeDtypeStruct((n, *pieces[0].shape), BF16),
    )(ids, *pieces)


def exchange(x, distance):
    n = lax.axis_size("head")
    return lax.ppermute(x, "head", [(i, i ^ distance) for i in range(n)])


def shift(x, distance, only=None):
    n = lax.axis_size("seq")
    route = [
        (i, i + distance)
        for i in range(n)
        if 0 <= i + distance < n and (only is None or i % 2 == only)
    ]
    return lax.ppermute(x, "seq", route)


def swap_pairs(x):
    n = lax.axis_size("seq")
    return lax.ppermute(x, "seq", [(i, i ^ 1) for i in range(n) if i ^ 1 < n])


def per_device(queries, keys, values, doc_ids):
    seq_index = lax.axis_index("seq")
    head_index = lax.axis_index("head")
    n_head = lax.axis_size("head")
    tile, q_heads, width = queries.shape
    kv_heads = keys.shape[1]
    groups = kv_heads // n_head
    local_heads = q_heads // n_head
    per_group = local_heads // groups
    block = tile * n_head
    reach = MAXDOC // block

    packed = jnp.stack([keys, values]).reshape(2, tile, n_head, groups, width)
    packed = packed.transpose(2, 0, 3, 1, 4)
    info_ids = jnp.stack([seq_index, head_index]).astype(jnp.int32)
    pieces = [lax.dynamic_index_in_dim(packed, head_index ^ d, 0, keepdims=False) for d in range(n_head)]
    pieces = [piece if d == 0 else exchange(piece, d) for d, piece in enumerate(pieces)]
    near = lax.dynamic_slice_in_dim(queries, (head_index ^ 1) * local_heads, local_heads, axis=1)
    pairs = [
        lax.dynamic_slice_in_dim(
            queries, (head_index ^ d) // 2 * 2 * local_heads, 2 * local_heads, axis=1
        )
        for d in range(2, n_head, 2)
    ]
    pieces, near, pairs = lax.optimization_barrier((pieces, near, pairs))
    own = assemble(info_ids, pieces)
    own, doc_ids = lax.optimization_barrier((own, doc_ids))

    two = shift(own, 2)
    odd_one = shift(own, 1, only=0)
    four = shift(two, 2)
    swapped = swap_pairs(two)
    even_three = shift(two, 1, only=1)
    blocks = (own, two, odd_one, four, swapped, even_three)

    q_doc = lax.dynamic_slice_in_dim(doc_ids, seq_index * block, block)
    start = jnp.sum((doc_ids[None, :] < q_doc[:, None]).astype(jnp.int32), axis=1)
    start = start - (seq_index - reach) * block
    start_row = jnp.repeat(start, per_group).reshape(n_head, 1, tile * per_group)
    info = jnp.concatenate([info_ids, start])

    first_qs = [queries, exchange(near, 1)]
    state = attend(info, start_row, first_qs, groups, blocks[:3], (), False, local_heads)
    other_qs = []
    for d, pair in zip(range(2, n_head, 2), pairs):
        pair = exchange(pair, d)
        other = lax.dynamic_slice_in_dim(
            pair, (1 - head_index % 2) * local_heads, local_heads, axis=1
        )
        other, _, state = lax.optimization_barrier((other, blocks, state))
        other_qs += [pair, exchange(other, 1)]
    out = attend(
        info, start_row, first_qs + other_qs, groups, blocks, state, True, local_heads
    )
    return out


def solution(mesh):
    in_specs = (
        P(("seq", "head"), None, None),
        P(("seq", "head"), None, None),
        P(("seq", "head"), None, None),
        P(),
    )
    out_specs = P("seq", "head", None)
    return jax.shard_map(
        per_device, mesh=mesh, in_specs=in_specs, out_specs=out_specs, check_vma=False
    )
```

```python
import math

import jax
import jax.numpy as jnp
from jax import lax
from jax.experimental import pallas as pl
from jax.experimental.pallas import tpu as pltpu
from jax.sharding import PartitionSpec as P

MAXDOC = 2048
EXTRA = 16
NEG = -1e30
F32 = jnp.float32
BF16 = jnp.bfloat16


def round_up(value, step):
    return (value + step - 1) // step * step


def fold_rows(op, x):
    out = x[:8]
    for c in range(1, x.shape[0] // 8):
        out = op(out, x[c * 8 : c * 8 + 8])
    return out


def attend_kernel(info, *refs, n_q, n_kv, n_carried, last, n_groups, width):
    count = n_q * n_groups
    refs = list(refs)
    start_ref = refs.pop(0)
    q_in = [refs.pop(0) for _ in range(n_q)]
    kv_in = [refs.pop(0) for _ in range(n_kv)]
    state_in = [refs.pop(0) for _ in range(2 if n_carried else 0)]
    out_refs = [refs.pop(0) for _ in range(1 if last else 2)]
    q_buf, k_buf, v_buf, vt_buf, s_buf, p_buf, m_buf, m_old, m_in, f_buf, acc, state, o_buf, sems, q_sems, o_sems = refs
    tile, per_group = q_buf.shape[1], q_buf.shape[2]
    rows = tile * per_group
    n_head, _, _, piece, _ = kv_in[0].shape
    block = n_head * piece
    reach = MAXDOC // block
    col = min(256, rows)
    chunk = 128
    col_tokens = col // per_group
    exp_scale = math.log2(math.e) / math.sqrt(width)
    odd = info[0] % 2 == 1
    head = info[1]

    def copies(source, slot, sem):
        return [
            pltpu.make_async_copy(
                source.at[:, which, g],
                buf.at[g, pl.ds((slot + 1) * n_head, n_head)],
                sems.at[sem, g * 2 + which],
            )
            for g in range(n_groups)
            for which, buf in ((0, k_buf), (1, v_buf))
        ]

    loads, later = [], []
    for t in range(count):
        source, g = q_in[t // n_groups], t % n_groups
        part = head if t < n_groups else 0
        first_head = part * n_groups * per_group + g * per_group
        later.append(
            pltpu.make_async_copy(
                source.at[:, pl.ds(first_head, per_group)], q_buf.at[t], q_sems.at[0, t]
            )
        )
    loads += copies(kv_in[0], reach, 0) + copies(kv_in[1], reach - 2, 1)
    at_odd = copies(kv_in[2], reach - 1, 2)
    at_even = []
    slots = [reach, reach - 1, reach - 2]
    if last:
        four, swapped, even_three = kv_in[3:]
        loads += copies(four, reach - 4, 3)
        at_odd += copies(swapped, reach - 3, 4)
        at_even += copies(swapped, reach - 1, 2) + copies(even_three, reach - 3, 4)
        slots = range(reach + 1)

    def sums_of(t):
        return pltpu.make_async_copy(state_in[0].at[t], state.at[t], q_sems.at[1, t])

    m_in[...] = jnp.full(m_in.shape, NEG, F32)
    if n_carried:
        loads.append(
            pltpu.make_async_copy(state_in[1], m_in.at[pl.ds(0, n_carried)], sems.at[5, 0])
        )
        later = [c for t, q in enumerate(later) for c in [q] + ([sums_of(t)] if t < n_carried else [])]
    for c in loads:
        c.start()
    for wanted, parity in ((at_odd, odd), (at_even, jnp.logical_not(odd))):

        @pl.when(parity)
        def _():
            for c in wanted:
                c.start()

    for c in later:
        c.start()
    s_buf[...] = jnp.full(s_buf.shape, NEG, F32)
    p_buf[...] = jnp.zeros(p_buf.shape, BF16)
    for buf in (m_buf, m_old, acc):
        buf[...] = jnp.zeros(buf.shape, F32)
    f_buf[...] = jnp.ones(f_buf.shape, F32)
    vt_buf[:, width:, :] = jnp.ones((n_groups, EXTRA, vt_buf.shape[2]), BF16)
    vt_buf[:, :, 0:block] = jnp.zeros((n_groups, width + EXTRA, block), BF16)
    for wanted, parity in ((at_odd, odd), (at_even, jnp.logical_not(odd))):

        @pl.when(parity)
        def _():
            for c in wanted:
                c.wait()

    for c in loads:
        c.wait()
    for g in range(n_groups):
        for b in slots:
            part = v_buf[g, (b + 1) * n_head : (b + 2) * n_head].reshape(block, width)
            vt_buf[g, 0:width, (b + 1) * block : (b + 2) * block] = part.T
    if n_carried:
        sums_of(0).wait()
        acc[...] = state[0]

    def first_of(t):
        return (head ^ (t // n_groups)) * tile

    def n_steps(t):
        back = reach - info[2 + first_of(t)] // block
        if not last:
            return 1 + jnp.where(odd, jnp.minimum(back, 2), jnp.minimum(back // 2, 1))
        n_even = jnp.where(back >= 3, back - 1, jnp.minimum(back, 1))
        carried = jnp.maximum(jnp.where(odd, back - 2, n_even), 1)
        below_top = top_of(t) - info[2 + first_of(t)]
        return jnp.where(t < n_carried, carried, (below_top + block - 1) // block)

    def top_of(t):
        return (reach * block + first_of(t) + tile + 127) // 128 * 128

    def key_of(t, j):
        if not last:
            return (reach - jnp.where(odd, j, 2 * j)) * block
        back = jnp.where(odd, j + 3, jnp.where(j == 0, 1, j + 2))
        return jnp.where(t < n_carried, (reach - back) * block, top_of(t) - (j + 1) * block)

    def body(qk, ex, pv, mask):
        (t, j), (_, _), (t2, j2) = qk, ex, pv
        first = first_of(t)
        g, g2 = t % n_groups, t2 % n_groups
        u0 = key_of(t, j)
        k_first = (u0 + block) // piece
        v_first = pl.multiple_of(key_of(t2, j2) + block, 128)
        vt = vt_buf[g2, :, pl.ds(v_first, block)]
        opening = j == 0
        for b in range(rows // col):
            r = pl.ds(b * col, col)
            f = f_buf[:, r]
            acc[:, r] = acc[:, r] * f + jnp.dot(vt, p_buf[:, r], preferred_element_type=F32)
            m = m_buf[:, r]
            f_buf[:, r] = jnp.exp2(m_old[:, r] - m)
            q = q_buf[t, pl.ds(b * col_tokens, col_tokens)].reshape(col, width)
            top = None
            for a in range(block // chunk):
                k = pl.ds(a * chunk, chunk)
                p = jnp.exp2(s_buf[k, r] * exp_scale - m)
                p_buf[k, r] = p.astype(BF16)
                per = chunk // piece
                kk = k_buf[g, pl.ds(k_first + a * per, per)].reshape(chunk, width)
                s = lax.dot_general(kk, q, (((1,), (1,)), ((), ())), preferred_element_type=F32)
                ok = None
                u = a * chunk + lax.broadcasted_iota(jnp.int32, (chunk, col), 0)
                if mask in ("start", "both"):
                    ok = u >= start_ref[first // tile, :, r] - u0
                if mask in ("end", "both") and (not last or a == block // chunk - 1):
                    lane = lax.broadcasted_iota(jnp.int32, (1, col), 1)
                    at = reach * block + first - u0 + b * col_tokens + lane // per_group
                    ok = u <= at if ok is None else ok & (u <= at)
                if ok is not None:
                    s = jnp.where(ok, s, NEG)
                s_buf[k, r] = s
                part = fold_rows(jnp.maximum, s)
                top = part if top is None else jnp.maximum(top, part)
            before = jnp.where(opening, m_in[t, :, r], m)
            m_old[:, r] = before
            m_buf[:, r] = jnp.maximum(before, jnp.max(top, axis=0, keepdims=True) * exp_scale)

    def results(t):
        if not last:
            return [
                pltpu.make_async_copy(state.at[t], out_refs[0].at[t], o_sems.at[0, t]),
                pltpu.make_async_copy(m_in.at[t], out_refs[1].at[t], o_sems.at[1, t]),
            ]
        heads = pl.ds((t % n_groups) * per_group, per_group)
        target = out_refs[0].at[pl.ds(first_of(t), tile), heads]
        return [pltpu.make_async_copy(o_buf.at[t], target, o_sems.at[0, t])]

    def finish(t, top):
        if last:
            for b in range(rows // col):
                r = pl.ds(b * col, col)
                inverse = 1.0 / acc[width : width + 1, r]
                o = (acc[0:width, r] * inverse).astype(BF16).T
                o_buf[t, pl.ds(b * col_tokens, col_tokens)] = o.reshape(col_tokens, per_group, width)
            if n_carried:

                @pl.when(t + 1 < n_carried)
                def _():
                    sums_of(t + 1).wait()
                    acc[...] = state[t + 1]
        else:
            state[t] = acc[...]
        for c in results(t):
            c.start()

    total_steps = n_steps(0)
    for t in range(1, count):
        total_steps = total_steps + n_steps(t)

    def loop(s, carry):
        t, j, t1, j1, t2, j2 = carry
        hi_start = info[2 + first_of(t) + tile - 1]
        at_start = key_of(t, j) < hi_start
        at_end = key_of(t, j) + block > reach * block + first_of(t)
        not_start, not_end = jnp.logical_not(at_start), jnp.logical_not(at_end)
        cases = {
            "none": not_start & not_end,
            "start": at_start & not_end,
            "end": not_start & at_end,
            "both": at_start & at_end,
        }
        if not last:
            @pl.when((s >= 1) & (j1 == n_steps(t1) - 1))
            def _():
                m_in[t1] = m_buf[...]

        @pl.when((j == 0) & (s < total_steps))
        def _():
            pltpu.make_async_copy(
                q_in[0].at[:, pl.ds(0, per_group)], q_buf.at[t], q_sems.at[0, t]
            ).wait()

        for mask, case in cases.items():

            @pl.when(case)
            def _():
                body((t, j), (t1, j1), (t2, j2), mask)

        @pl.when((s >= 2) & (j2 == n_steps(t2) - 1))
        def _():
            finish(t2, None)

        over = j == n_steps(t) - 1
        t_next = jnp.where(over, jnp.minimum(t + 1, count - 1), t)
        j_next = jnp.where(over, 0, j + 1)
        return t_next, j_next, t, j, t1, j1

    zero = jnp.int32(0)
    lax.fori_loop(0, total_steps + 2, loop, (zero,) * 6)
    for t in range(count):
        for c in results(t):
            c.wait()


def attend(info, start_row, qs, n_groups, kv_blocks, state, last, local_heads):
    tile, _, width = qs[0].shape
    n_head, _, _, piece, _ = kv_blocks[0].shape
    block = n_head * piece
    per_group = local_heads // n_groups
    rows = tile * per_group
    keys = MAXDOC + 2 * block
    count = len(qs) * n_groups
    n_carried = state[0].shape[0] if state else 0
    n_state = n_carried if last else count

    def kernel(*refs):
        attend_kernel(
            *refs,
            n_q=len(qs),
            n_kv=len(kv_blocks),
            n_carried=n_carried,
            last=last,
            n_groups=n_groups,
            width=width,
        )

    any_spec = pl.BlockSpec(memory_space=pl.ANY)
    if last:
        out_shape = jax.ShapeDtypeStruct((block, local_heads, width), BF16)
    else:
        out_shape = (
            jax.ShapeDtypeStruct((count, width + EXTRA, rows), F32),
            jax.ShapeDtypeStruct((count, 1, rows), F32),
        )
    grid_spec = pltpu.PrefetchScalarGridSpec(
        num_scalar_prefetch=1,
        grid=(1,),
        in_specs=[pl.BlockSpec(memory_space=pltpu.VMEM)]
        + [any_spec] * (len(qs) + len(kv_blocks) + len(state)),
        out_specs=any_spec if last else (any_spec, any_spec),
        scratch_shapes=[
            pltpu.VMEM((count, tile, per_group, width), BF16),
            pltpu.VMEM((n_groups, keys // piece, piece, width), BF16),
            pltpu.VMEM((n_groups, keys // piece, piece, width), BF16),
            pltpu.VMEM((n_groups, width + EXTRA, keys), BF16),
            pltpu.VMEM((block, rows), F32),
            pltpu.VMEM((block, rows), BF16),
            pltpu.VMEM((1, rows), F32),
            pltpu.VMEM((1, rows), F32),
            pltpu.VMEM((count, 1, rows), F32),
            pltpu.VMEM((1, rows), F32),
            pltpu.VMEM((width + EXTRA, rows), F32),
            pltpu.VMEM((n_state, width + EXTRA, rows), F32),
            pltpu.VMEM((count, tile, per_group, width), BF16),
            pltpu.SemaphoreType.DMA((6, 2 * n_groups)),
            pltpu.SemaphoreType.DMA((2, count)),
            pltpu.SemaphoreType.DMA((2, count)),
        ],
    )
    return pl.pallas_call(
        kernel,
        grid_spec=grid_spec,
        out_shape=out_shape,
        compiler_params=pltpu.CompilerParams(vmem_limit_bytes=63 * 2**20),
        cost_estimate=pl.CostEstimate(
            flops=2**20 if last else 6 * 10**9, bytes_accessed=2**20, transcendentals=0
        ),
    )(info, start_row, *qs, *kv_blocks, *state)


def assemble(ids, pieces):
    n = len(pieces)

    def kernel(ids, *refs):
        for d in range(n):
            refs[n][ids[1] ^ d] = refs[d][...]

    return pl.pallas_call(
        kernel,
        grid_spec=pltpu.PrefetchScalarGridSpec(
            num_scalar_prefetch=1,
            grid=(1,),
            in_specs=[pl.BlockSpec(memory_space=pltpu.VMEM)] * n,
            out_specs=pl.BlockSpec(memory_space=pltpu.VMEM),
        ),
        out_shape=jax.ShapeDtypeStruct((n, *pieces[0].shape), BF16),
    )(ids, *pieces)


def exchange(x, distance):
    n = lax.axis_size("head")
    return lax.ppermute(x, "head", [(i, i ^ distance) for i in range(n)])


def shift(x, distance, only=None):
    n = lax.axis_size("seq")
    route = [
        (i, i + distance)
        for i in range(n)
        if 0 <= i + distance < n and (only is None or i % 2 == only)
    ]
    return lax.ppermute(x, "seq", route)


def swap_pairs(x):
    n = lax.axis_size("seq")
    return lax.ppermute(x, "seq", [(i, i ^ 1) for i in range(n) if i ^ 1 < n])


def per_device(queries, keys, values, doc_ids):
    seq_index = lax.axis_index("seq")
    head_index = lax.axis_index("head")
    n_head = lax.axis_size("head")
    tile, q_heads, width = queries.shape
    kv_heads = keys.shape[1]
    groups = kv_heads // n_head
    local_heads = q_heads // n_head
    per_group = local_heads // groups
    block = tile * n_head
    reach = MAXDOC // block

    packed = jnp.stack([keys, values]).reshape(2, tile, n_head, groups, width)
    packed = packed.transpose(2, 0, 3, 1, 4)
    info_ids = jnp.stack([seq_index, head_index]).astype(jnp.int32)
    pieces = [lax.dynamic_index_in_dim(packed, head_index ^ d, 0, keepdims=False) for d in range(n_head)]
    pieces = [piece if d == 0 else exchange(piece, d) for d, piece in enumerate(pieces)]
    slices = [
        lax.dynamic_slice_in_dim(queries, (head_index ^ d) * local_heads, local_heads, axis=1)
        for d in range(1, n_head)
    ]
    pieces, slices = lax.optimization_barrier((pieces, slices))
    own = assemble(info_ids, pieces)
    own, doc_ids = lax.optimization_barrier((own, doc_ids))

    two = shift(own, 2)
    odd_one = shift(own, 1, only=0)
    four = shift(two, 2)
    swapped = swap_pairs(two)
    even_three = shift(two, 1, only=1)
    blocks = (own, two, odd_one, four, swapped, even_three)

    q_doc = lax.dynamic_slice_in_dim(doc_ids, seq_index * block, block)
    start = jnp.sum((doc_ids[None, :] < q_doc[:, None]).astype(jnp.int32), axis=1)
    start = start - (seq_index - reach) * block
    start_row = jnp.repeat(start, per_group).reshape(n_head, 1, tile * per_group)
    info = jnp.concatenate([info_ids, start])

    first_qs = [queries, exchange(slices[0], 1)]
    other_qs = []
    for d in range(2, n_head):
        q = slices[d - 1]
        if other_qs:
            q, _ = lax.optimization_barrier((q, other_qs[-1]))
        other_qs.append(exchange(q, d))
    state = attend(info, start_row, first_qs, groups, blocks[:3], (), False, local_heads)
    out = attend(
        info, start_row, first_qs + other_qs, groups, blocks, state, True, local_heads
    )
    return out


def solution(mesh):
    in_specs = (
        P(("seq", "head"), None, None),
        P(("seq", "head"), None, None),
        P(("seq", "head"), None, None),
        P(),
    )
    out_specs = P("seq", "head", None)
    return jax.shard_map(
        per_device, mesh=mesh, in_specs=in_specs, out_specs=out_specs, check_vma=False
    )
```

```python
import math

import jax
import jax.numpy as jnp
from jax import lax
from jax.experimental import pallas as pl
from jax.experimental.pallas import tpu as pltpu
from jax.sharding import PartitionSpec as P

MAXDOC = 2048
EXTRA = 16
NEG = -1e30
F32 = jnp.float32
BF16 = jnp.bfloat16


def round_up(value, step):
    return (value + step - 1) // step * step


def fold_rows(op, x):
    out = x[:8]
    for c in range(1, x.shape[0] // 8):
        out = op(out, x[c * 8 : c * 8 + 8])
    return out


def attend_kernel(info, *refs, n_q, n_kv, n_carried, last, n_groups, width):
    count = n_q * n_groups
    refs = list(refs)
    start_ref = refs.pop(0)
    q_in = [refs.pop(0) for _ in range(n_q)]
    kv_in = [refs.pop(0) for _ in range(n_kv)]
    state_in = [refs.pop(0) for _ in range(2 if n_carried else 0)]
    out_refs = [refs.pop(0) for _ in range(1 if last else 2)]
    q_buf, k_buf, v_buf, vt_buf, s_buf, p_buf, m_buf, m_old, m_in, f_buf, acc, state, o_buf, sems, q_sems, o_sems = refs
    tile, per_group = q_buf.shape[1], q_buf.shape[2]
    rows = tile * per_group
    n_head, _, _, piece, _ = kv_in[0].shape
    block = n_head * piece
    reach = MAXDOC // block
    col = min(256, rows)
    chunk = 128
    col_tokens = col // per_group
    exp_scale = math.log2(math.e) / math.sqrt(width)
    odd = info[0] % 2 == 1
    head = info[1]

    def copies(source, slot, sem):
        return [
            pltpu.make_async_copy(
                source.at[:, which, g],
                buf.at[g, pl.ds((slot + 1) * n_head, n_head)],
                sems.at[sem, g * 2 + which],
            )
            for g in range(n_groups)
            for which, buf in ((0, k_buf), (1, v_buf))
        ]

    loads, later = [], []
    for t in range(count):
        source, g = q_in[t // n_groups], t % n_groups
        part = head if t < n_groups else 0
        first_head = part * n_groups * per_group + g * per_group
        later.append(
            pltpu.make_async_copy(
                source.at[:, pl.ds(first_head, per_group)], q_buf.at[t], q_sems.at[0, t]
            )
        )
    loads += copies(kv_in[0], reach, 0) + copies(kv_in[1], reach - 2, 1)
    at_odd = copies(kv_in[2], reach - 1, 2)
    at_even = []
    slots = [reach, reach - 1, reach - 2]
    if last:
        four, swapped, even_three = kv_in[3:]
        loads += copies(four, reach - 4, 3)
        at_odd += copies(swapped, reach - 3, 4)
        at_even += copies(swapped, reach - 1, 2) + copies(even_three, reach - 3, 4)
        slots = range(reach + 1)

    def sums_of(t):
        return pltpu.make_async_copy(state_in[0].at[t], state.at[t], q_sems.at[1, t])

    m_in[...] = jnp.full(m_in.shape, NEG, F32)
    if n_carried:
        loads.append(
            pltpu.make_async_copy(state_in[1], m_in.at[pl.ds(0, n_carried)], sems.at[5, 0])
        )
        later = [c for t, q in enumerate(later) for c in [q] + ([sums_of(t)] if t < n_carried else [])]
    for c in loads:
        c.start()
    for wanted, parity in ((at_odd, odd), (at_even, jnp.logical_not(odd))):

        @pl.when(parity)
        def _():
            for c in wanted:
                c.start()

    for c in later:
        c.start()
    s_buf[...] = jnp.full(s_buf.shape, NEG, F32)
    p_buf[...] = jnp.zeros(p_buf.shape, BF16)
    for buf in (m_buf, m_old, acc):
        buf[...] = jnp.zeros(buf.shape, F32)
    f_buf[...] = jnp.ones(f_buf.shape, F32)
    vt_buf[:, width:, :] = jnp.ones((n_groups, EXTRA, vt_buf.shape[2]), BF16)
    vt_buf[:, :, 0:block] = jnp.zeros((n_groups, width + EXTRA, block), BF16)
    for wanted, parity in ((at_odd, odd), (at_even, jnp.logical_not(odd))):

        @pl.when(parity)
        def _():
            for c in wanted:
                c.wait()

    for c in loads:
        c.wait()
    for g in range(n_groups):
        for b in slots:
            part = v_buf[g, (b + 1) * n_head : (b + 2) * n_head].reshape(block, width)
            vt_buf[g, 0:width, (b + 1) * block : (b + 2) * block] = part.T
    if n_carried:
        sums_of(0).wait()
        acc[...] = state[0]

    def first_of(t):
        return (head ^ (t // n_groups)) * tile

    def n_steps(t):
        back = reach - info[2 + first_of(t)] // block
        if not last:
            return 1 + jnp.where(odd, jnp.minimum(back, 2), jnp.minimum(back // 2, 1))
        n_even = jnp.where(back >= 3, back - 1, jnp.minimum(back, 1))
        carried = jnp.maximum(jnp.where(odd, back - 2, n_even), 1)
        below_top = top_of(t) - info[2 + first_of(t)]
        return jnp.where(t < n_carried, carried, (below_top + block - 1) // block)

    def top_of(t):
        return (reach * block + first_of(t) + tile + 127) // 128 * 128

    def key_of(t, j):
        if not last:
            return (reach - jnp.where(odd, j, 2 * j)) * block
        back = jnp.where(odd, j + 3, jnp.where(j == 0, 1, j + 2))
        return jnp.where(t < n_carried, (reach - back) * block, top_of(t) - (j + 1) * block)

    def body(qk, ex, pv, mask):
        (t, j), (_, _), (t2, j2) = qk, ex, pv
        first = first_of(t)
        g, g2 = t % n_groups, t2 % n_groups
        u0 = key_of(t, j)
        k_first = (u0 + block) // piece
        v_first = pl.multiple_of(key_of(t2, j2) + block, 128)
        vt = vt_buf[g2, :, pl.ds(v_first, block)]
        opening = j == 0
        for b in range(rows // col):
            r = pl.ds(b * col, col)
            f = f_buf[:, r]
            acc[:, r] = acc[:, r] * f + jnp.dot(vt, p_buf[:, r], preferred_element_type=F32)
            m = m_buf[:, r]
            f_buf[:, r] = jnp.exp2(m_old[:, r] - m)
            q = q_buf[t, pl.ds(b * col_tokens, col_tokens)].reshape(col, width)
            top = None
            for a in range(block // chunk):
                k = pl.ds(a * chunk, chunk)
                p = jnp.exp2(s_buf[k, r] * exp_scale - m)
                p_buf[k, r] = p.astype(BF16)
                if mask == "drain":
                    continue
                per = chunk // piece
                kk = k_buf[g, pl.ds(k_first + a * per, per)].reshape(chunk, width)
                s = lax.dot_general(kk, q, (((1,), (1,)), ((), ())), preferred_element_type=F32)
                ok = None
                u = a * chunk + lax.broadcasted_iota(jnp.int32, (chunk, col), 0)
                if mask in ("start", "both"):
                    ok = u >= start_ref[first // tile, :, r] - u0
                if mask in ("end", "both") and (not last or a == block // chunk - 1):
                    lane = lax.broadcasted_iota(jnp.int32, (1, col), 1)
                    at = reach * block + first - u0 + b * col_tokens + lane // per_group
                    ok = u <= at if ok is None else ok & (u <= at)
                if ok is not None:
                    s = jnp.where(ok, s, NEG)
                s_buf[k, r] = s
                part = fold_rows(jnp.maximum, s)
                top = part if top is None else jnp.maximum(top, part)
            if mask == "drain":
                continue
            before = jnp.where(opening, m_in[t, :, r], m)
            m_old[:, r] = before
            m_buf[:, r] = jnp.maximum(before, jnp.max(top, axis=0, keepdims=True) * exp_scale)

    def results(t):
        if not last:
            return [
                pltpu.make_async_copy(state.at[t], out_refs[0].at[t], o_sems.at[0, t]),
                pltpu.make_async_copy(m_in.at[t], out_refs[1].at[t], o_sems.at[1, t]),
            ]
        heads = pl.ds((t % n_groups) * per_group, per_group)
        target = out_refs[0].at[pl.ds(first_of(t), tile), heads]
        return [pltpu.make_async_copy(o_buf.at[t], target, o_sems.at[0, t])]

    def finish(t, top):
        if last:
            for b in range(rows // col):
                r = pl.ds(b * col, col)
                inverse = 1.0 / acc[width : width + 1, r]
                o = (acc[0:width, r] * inverse).astype(BF16).T
                o_buf[t, pl.ds(b * col_tokens, col_tokens)] = o.reshape(col_tokens, per_group, width)
            if n_carried:

                @pl.when(t + 1 < n_carried)
                def _():
                    sums_of(t + 1).wait()
                    acc[...] = state[t + 1]
        else:
            state[t] = acc[...]
        for c in results(t):
            c.start()

    total_steps = n_steps(0)
    for t in range(1, count):
        total_steps = total_steps + n_steps(t)

    def loop(s, carry):
        t, j, t1, j1, t2, j2 = carry
        hi_start = info[2 + first_of(t) + tile - 1]
        at_start = key_of(t, j) < hi_start
        at_end = key_of(t, j) + block > reach * block + first_of(t)
        not_start, not_end = jnp.logical_not(at_start), jnp.logical_not(at_end)
        more = s < total_steps
        cases = {
            "none": not_start & not_end & more,
            "start": at_start & not_end & more,
            "end": not_start & at_end & more,
            "both": at_start & at_end & more,
            "drain": s >= total_steps,
        }
        if not last:
            @pl.when((s >= 1) & (j1 == n_steps(t1) - 1))
            def _():
                m_in[t1] = m_buf[...]

        @pl.when((j == 0) & (s < total_steps))
        def _():
            pltpu.make_async_copy(
                q_in[0].at[:, pl.ds(0, per_group)], q_buf.at[t], q_sems.at[0, t]
            ).wait()

        for mask, case in cases.items():

            @pl.when(case)
            def _():
                body((t, j), (t1, j1), (t2, j2), mask)

        @pl.when((s >= 2) & (j2 == n_steps(t2) - 1))
        def _():
            finish(t2, None)

        over = j == n_steps(t) - 1
        t_next = jnp.where(over, jnp.minimum(t + 1, count - 1), t)
        j_next = jnp.where(over, 0, j + 1)
        return t_next, j_next, t, j, t1, j1

    zero = jnp.int32(0)
    lax.fori_loop(0, total_steps + 2, loop, (zero,) * 6)
    for t in range(count):
        for c in results(t):
            c.wait()


def attend(info, start_row, qs, n_groups, kv_blocks, state, last, local_heads):
    tile, _, width = qs[0].shape
    n_head, _, _, piece, _ = kv_blocks[0].shape
    block = n_head * piece
    per_group = local_heads // n_groups
    rows = tile * per_group
    keys = MAXDOC + 2 * block
    count = len(qs) * n_groups
    n_carried = state[0].shape[0] if state else 0
    n_state = n_carried if last else count

    def kernel(*refs):
        attend_kernel(
            *refs,
            n_q=len(qs),
            n_kv=len(kv_blocks),
            n_carried=n_carried,
            last=last,
            n_groups=n_groups,
            width=width,
        )

    any_spec = pl.BlockSpec(memory_space=pl.ANY)
    if last:
        out_shape = jax.ShapeDtypeStruct((block, local_heads, width), BF16)
    else:
        out_shape = (
            jax.ShapeDtypeStruct((count, width + EXTRA, rows), F32),
            jax.ShapeDtypeStruct((count, 1, rows), F32),
        )
    grid_spec = pltpu.PrefetchScalarGridSpec(
        num_scalar_prefetch=1,
        grid=(1,),
        in_specs=[pl.BlockSpec(memory_space=pltpu.VMEM)]
        + [any_spec] * (len(qs) + len(kv_blocks) + len(state)),
        out_specs=any_spec if last else (any_spec, any_spec),
        scratch_shapes=[
            pltpu.VMEM((count, tile, per_group, width), BF16),
            pltpu.VMEM((n_groups, keys // piece, piece, width), BF16),
            pltpu.VMEM((n_groups, keys // piece, piece, width), BF16),
            pltpu.VMEM((n_groups, width + EXTRA, keys), BF16),
            pltpu.VMEM((block, rows), F32),
            pltpu.VMEM((block, rows), BF16),
            pltpu.VMEM((1, rows), F32),
            pltpu.VMEM((1, rows), F32),
            pltpu.VMEM((count, 1, rows), F32),
            pltpu.VMEM((1, rows), F32),
            pltpu.VMEM((width + EXTRA, rows), F32),
            pltpu.VMEM((n_state, width + EXTRA, rows), F32),
            pltpu.VMEM((count, tile, per_group, width), BF16),
            pltpu.SemaphoreType.DMA((6, 2 * n_groups)),
            pltpu.SemaphoreType.DMA((2, count)),
            pltpu.SemaphoreType.DMA((2, count)),
        ],
    )
    return pl.pallas_call(
        kernel,
        grid_spec=grid_spec,
        out_shape=out_shape,
        compiler_params=pltpu.CompilerParams(vmem_limit_bytes=63 * 2**20),
        cost_estimate=pl.CostEstimate(
            flops=2**20 if last else 6 * 10**9, bytes_accessed=2**20, transcendentals=0
        ),
    )(info, start_row, *qs, *kv_blocks, *state)


def assemble(ids, pieces):
    n = len(pieces)

    def kernel(ids, *refs):
        for d in range(n):
            refs[n][ids[1] ^ d] = refs[d][...]

    return pl.pallas_call(
        kernel,
        grid_spec=pltpu.PrefetchScalarGridSpec(
            num_scalar_prefetch=1,
            grid=(1,),
            in_specs=[pl.BlockSpec(memory_space=pltpu.VMEM)] * n,
            out_specs=pl.BlockSpec(memory_space=pltpu.VMEM),
        ),
        out_shape=jax.ShapeDtypeStruct((n, *pieces[0].shape), BF16),
    )(ids, *pieces)


def exchange(x, distance):
    n = lax.axis_size("head")
    return lax.ppermute(x, "head", [(i, i ^ distance) for i in range(n)])


def shift(x, distance, only=None):
    n = lax.axis_size("seq")
    route = [
        (i, i + distance)
        for i in range(n)
        if 0 <= i + distance < n and (only is None or i % 2 == only)
    ]
    return lax.ppermute(x, "seq", route)


def swap_pairs(x):
    n = lax.axis_size("seq")
    return lax.ppermute(x, "seq", [(i, i ^ 1) for i in range(n) if i ^ 1 < n])


def per_device(queries, keys, values, doc_ids):
    seq_index = lax.axis_index("seq")
    head_index = lax.axis_index("head")
    n_head = lax.axis_size("head")
    tile, q_heads, width = queries.shape
    kv_heads = keys.shape[1]
    groups = kv_heads // n_head
    local_heads = q_heads // n_head
    per_group = local_heads // groups
    block = tile * n_head
    reach = MAXDOC // block

    packed = jnp.stack([keys, values]).reshape(2, tile, n_head, groups, width)
    packed = packed.transpose(2, 0, 3, 1, 4)
    info_ids = jnp.stack([seq_index, head_index]).astype(jnp.int32)
    pieces = [lax.dynamic_index_in_dim(packed, head_index ^ d, 0, keepdims=False) for d in range(n_head)]
    pieces = [piece if d == 0 else exchange(piece, d) for d, piece in enumerate(pieces)]
    slices = [
        lax.dynamic_slice_in_dim(queries, (head_index ^ d) * local_heads, local_heads, axis=1)
        for d in range(1, n_head)
    ]
    pieces, slices = lax.optimization_barrier((pieces, slices))
    own = assemble(info_ids, pieces)

    own, doc_ids = lax.optimization_barrier((own, doc_ids))
    q_doc = lax.dynamic_slice_in_dim(doc_ids, seq_index * block, block)
    start = jnp.sum((doc_ids[None, :] < q_doc[:, None]).astype(jnp.int32), axis=1)
    start = start - (seq_index - reach) * block
    start_row = jnp.repeat(start, per_group).reshape(n_head, 1, tile * per_group)
    info = jnp.concatenate([info_ids, start])
    to_odd, info, start_row = lax.optimization_barrier((own, info, start_row))

    two = shift(own, 2)
    odd_one = shift(to_odd, 1, only=0)
    four = shift(two, 2)
    swapped = swap_pairs(two)
    even_three = shift(two, 1, only=1)
    blocks = (own, two, odd_one, four, swapped, even_three)

    first_qs = [queries, exchange(slices[0], 1)]
    other_qs = []
    for d in range(2, n_head):
        q = slices[d - 1]
        if other_qs:
            q, _ = lax.optimization_barrier((q, other_qs[-1]))
        other_qs.append(exchange(q, d))
    state = attend(info, start_row, first_qs, groups, blocks[:3], (), False, local_heads)
    out = attend(
        info, start_row, first_qs + other_qs, groups, blocks, state, True, local_heads
    )
    return out


def solution(mesh):
    in_specs = (
        P(("seq", "head"), None, None),
        P(("seq", "head"), None, None),
        P(("seq", "head"), None, None),
        P(),
    )
    out_specs = P("seq", "head", None)
    return jax.shard_map(
        per_device, mesh=mesh, in_specs=in_specs, out_specs=out_specs, check_vma=False
    )
```
